32 devices in a mesh: member: 16 (over z, y, core), tile: 2 (over x).
Axes of the slice: x: 2, y: 2, z: 4, core: 2. Of those that a mesh axis runs over, the one named last changes fastest.
Arguments:
- ensemble: float32 [64, 128, 2048], P('member', 'tile'), may hold values from -6 to 6
- velocity: float32 [2, 128, 2048], P(None, 'tile'), may hold values from -0.45 to 0.45
- observed_column: int32 [128, 16, 32], P('tile', 'member'), may hold values from 0 to 127
- observation_slot_count: int32 [128, 16], P('tile', 'member'), may hold values from 1 to 32
- local_radius: int32 [128, 16], P('tile', 'member'), may hold values from 16 to 128
- observed_value: float32 [128, 16, 32], P('tile', 'member'), may hold values from -9 to 9
- error_variance: float32 [128, 16, 32], P('tile', 'member'), may hold values from 0.25 to 2
Outputs:
- analysis: float32 [64, 128, 2048], P('member', 'tile')
The draws below stay inside these ranges and needn't reach their ends.
All inputs are finite; a program needn't handle non-finite values.
Results may differ from the reference program's by a relative error of at most 0.0003.
Values sent between devices are 32-bit elements; how exact they have to be, the bound alone decides.
A program may use at most 128 MiB of HBM per device.

```python
import math
import jax
import jax.numpy as jnp
from jax import lax

ENS = 64
COLS = 128
NOBS = 32
SWEEPS = 6
NX = 128
NY = 2048
NYT = 16


def place_ends(array, stream_key, low, largest):
    longest = array.shape.index(max(array.shape))
    spots = []
    for shift in (0, 1):
        where = [jax.random.randint(jax.random.fold_in(stream_key, axis), (), 0, length) for axis, length in enumerate(array.shape)]
        where[longest] = (where[longest] + shift) % array.shape[longest]
        spots.append(tuple(where))
    return array.at[spots[0]].set(low).at[spots[1]].set(largest)


def level_of(key, extent, split, low, high):
    gain, own = 1.0, jax.random.fold_in(key, 6)
    for axis_at, shards_of in split:
        heights = jnp.exp(jax.random.uniform(jax.random.fold_in(own, axis_at), (shards_of,), jnp.float32, low / len(split), high / len(split)))
        gain = gain * jnp.repeat(heights, extent[axis_at] // shards_of).reshape([-1 if axis == axis_at else 1 for axis in range(len(extent))])
    return gain


def noise(rng, extent, width, limit, pieces=(), held_as=jnp.bfloat16):
    entries = jax.random.normal(rng, extent, jnp.float32) * width
    if len(pieces) > 0:
        entries = level_of(rng, extent, pieces, -0.22, 0.18) * entries
    return jnp.clip(entries, min=-limit, max=limit).astype(held_as)


def setup_inputs(seed: int = 0) -> dict:
    streams_of = jax.random.split(jax.random.key(seed), 8)
    ensemble = noise(streams_of[0], (ENS, NX, NY), 1.0, 6.0, ((0, 16), (1, 2)), jnp.float32)
    velocity = jnp.clip(jax.random.uniform(streams_of[1], (2, NX, NY), jnp.float32, -0.45, 0.45) * level_of(streams_of[1], (2, NX, NY), ((1, 2),), -0.4, 0.0), -0.45, 0.45)
    observed_column = place_ends(jax.random.randint(streams_of[2], (NX, NYT, NOBS), 0, COLS), jax.random.fold_in(streams_of[2], 1), 0, COLS - 1).astype(jnp.int32)
    observation_slot_count = place_ends(jax.random.randint(streams_of[3], (NX, NYT), 1, NOBS + 1), jax.random.fold_in(streams_of[3], 1), 1, NOBS).astype(jnp.int32)
    local_radius = place_ends(jax.random.randint(streams_of[4], (NX, NYT), 16, 129), jax.random.fold_in(streams_of[4], 1), 16, 128).astype(jnp.int32)
    observed_value = noise(streams_of[5], (NX, NYT, NOBS), 1.5, 9.0, ((0, 2), (1, 16)), jnp.float32)
    error_variance = jnp.clip(jnp.exp(math.log(2.0) - 2.0794415 * jax.random.uniform(streams_of[6], (NX, NYT, NOBS), jnp.float32) ** level_of(streams_of[6], (NX, NYT, NOBS), ((0, 2), (1, 16)), -0.2, 0.2)), 0.25, 2.0)
    return {"ensemble": ensemble, "velocity": velocity, "observed_column": observed_column, "observation_slot_count": observation_slot_count, "local_radius": local_radius, "observed_value": observed_value, "error_variance": error_variance}


def advect(extended):
    carried_quantity = extended[:-2]
    east_wind = extended[-2]
    north_wind = extended[-1]
    face_x = 0.5 * (east_wind[1:, 1:-1] + east_wind[:-1, 1:-1])
    flux_x = jnp.maximum(face_x, 0.0) * carried_quantity[:, :-1, 1:-1] + jnp.minimum(face_x, 0.0) * carried_quantity[:, 1:, 1:-1]
    face_y = 0.5 * (north_wind[1:-1, 1:] + north_wind[1:-1, :-1])
    flux_y = jnp.maximum(face_y, 0.0) * carried_quantity[:, 1:-1, :-1] + jnp.minimum(face_y, 0.0) * carried_quantity[:, 1:-1, 1:]
    return carried_quantity[:, 1:-1, 1:-1] - (flux_x[:, 1:] - flux_x[:, :-1]) - (flux_y[:, :, 1:] - flux_y[:, :, :-1])

def analyse(background, columns, tally_count, radii, values, variances):
    highest = lax.Precision.HIGHEST
    members = background.shape[0]
    average = lax.optimization_barrier(jnp.mean(background, axis=0))
    anomaly = background - average[None]
    indicator_matrix = (columns[:, :, None] == jnp.arange(COLS, dtype=jnp.int32)[None, None, :]).astype(jnp.float32)
    observed = jnp.einsum('ebc,bsc->ebs', background, indicator_matrix, precision=highest)
    observed_mean = lax.optimization_barrier(jnp.mean(observed, axis=0))
    spread = observed - observed_mean[None]
    slot_index = jnp.arange(columns.shape[1], dtype=jnp.int32)
    active = (slot_index[None, :] < tally_count[:, None]).astype(jnp.float32)
    offset = (columns.astype(jnp.float32) - 0.5 * (COLS - 1)) / radii.astype(jnp.float32)[:, None]
    weight = active / (1.0 + offset * offset) / variances
    scaled = spread * weight[None]
    identity = jnp.eye(members, dtype=jnp.float32)
    system = jnp.einsum('ebs,fbs->bef', scaled, spread, precision=highest) + (members - 1.0) * identity[None]
    frobenius = jnp.sqrt(lax.optimization_barrier(jnp.sum(system * system, axis=(1, 2))))
    root = system / frobenius[:, None, None]
    inverse_root = jnp.broadcast_to(identity, root.shape)
    for number in range(SWEEPS):
        factor = 1.5 * identity[None] - 0.5 * jnp.einsum('bij,bjk->bik', inverse_root, root, precision=highest)
        root = jnp.einsum('bij,bjk->bik', root, factor, precision=highest)
        inverse_root = jnp.einsum('bij,bjk->bik', factor, inverse_root, precision=highest)
    inverse_root = inverse_root / jnp.sqrt(frobenius)[:, None, None]
    innovation = values - observed_mean
    projected = jnp.einsum('ebs,bs->be', scaled, innovation, precision=highest)
    halfway = jnp.einsum('bij,bj->bi', inverse_root, projected, precision=highest)
    mean_weight = jnp.einsum('bij,bj->bi', inverse_root, halfway, precision=highest)
    transform = jnp.sqrt(members - 1.0) * inverse_root + mean_weight[:, :, None]
    return average[None] + jnp.einsum('bkj,kbc->jbc', transform, anomaly, precision=highest)

def reference(ensemble, velocity, observed_column, observation_slot_count, local_radius, observed_value, error_variance):

    def predict_single_member(carried_quantity):
        for number in range(2):
            stacked = jnp.concatenate([carried_quantity[None], velocity], axis=0)
            carried_quantity = advect(jnp.pad(stacked, ((0, 0), (1, 1), (1, 1))))[0]
        return carried_quantity
    predicted_state = lax.map(predict_single_member, ensemble)
    grouped_by_row = jnp.moveaxis(predicted_state, 1, 0)

    def row_step(packed):
        row_state, columns, tally_count, radii, values, variances = packed
        tile_state = row_state.reshape(ENS, NYT, COLS)
        result = analyse(tile_state, columns, tally_count, radii, values, variances)
        return result.reshape(ENS, NY)
    analysed = lax.map(row_step, (grouped_by_row, observed_column, observation_slot_count, local_radius, observed_value, error_variance))
    return jnp.moveaxis(analysed, 0, 1)
```

```python
import functools
import math

import jax
import jax.numpy as jnp
from jax import lax
from jax.experimental import pallas as pl
from jax.experimental.pallas import tpu as pltpu
from jax.sharding import PartitionSpec as P

COLS = 128
SWEEPS = 6
EDGE = 8
STRIP = 256
ROWS_PER_CHUNK = 16
PAIRS = 4


def split(x):
    high = x.astype(jnp.bfloat16)
    low = (x - high.astype(jnp.float32)).astype(jnp.bfloat16)
    return high, low


def product(a, b, dims=(((1,), (0,)), ((), ()))):
    dot = functools.partial(
        lax.dot_general, dimension_numbers=dims, preferred_element_type=jnp.float32
    )
    return dot(a[0], b[0]) + (dot(a[0], b[1]) + dot(a[1], b[0]))


def kernel(
    sizes,
    ensemble,
    velocity,
    columns_ref,
    count_ref,
    radius_ref,
    value_ref,
    variance_ref,
    out,
    extended,
    outgoing,
    gathered,
    analysed,
    column_lanes,
    weight_lanes,
    value_lanes,
    load_sem,
    halo_send,
    halo_recv,
    there_send,
    there_recv,
    there_own,
    back_send,
    back_recv,
    back_own,
):
    devices, bands, local, rows, width, step, slots = sizes
    members = devices * local
    chunks = rows // step
    me = lax.axis_index("member")
    band = lax.axis_index("tile")
    part = local * step
    body = pl.ds(COLS, width)

    loads = [
        pltpu.make_async_copy(
            ensemble, extended.at[pl.ds(0, local), pl.ds(EDGE, rows), body], load_sem.at[0]
        ),
        pltpu.make_async_copy(
            velocity, extended.at[pl.ds(local, 2), pl.ds(EDGE, rows), body], load_sem.at[1]
        ),
    ]
    for load in loads:
        load.start()

    barrier = pltpu.get_barrier_semaphore()

    @pl.loop(1, devices)
    def _(k):
        pl.semaphore_signal(barrier, inc=1, device_id={"member": lax.rem(me + k, devices)})

    @pl.when(band > 0)
    def _():
        pl.semaphore_signal(barrier, inc=1, device_id={"tile": band - 1})

    @pl.when(band < bands - 1)
    def _():
        pl.semaphore_signal(barrier, inc=1, device_id={"tile": band + 1})

    extended[:, :, 0:COLS] = jnp.zeros((local + 2, rows + 2 * EDGE, COLS), jnp.float32)
    extended[:, :, COLS + width :] = jnp.zeros((local + 2, rows + 2 * EDGE, COLS), jnp.float32)

    @pl.when(band == 0)
    def _():
        extended[:, 0:EDGE, COLS : COLS + width] = jnp.zeros((local + 2, EDGE, width), jnp.float32)

    @pl.when(band == bands - 1)
    def _():
        extended[:, EDGE + rows :, COLS : COLS + width] = jnp.zeros(
            (local + 2, EDGE, width), jnp.float32
        )

    def spread_lanes(x):
        return jnp.concatenate([x] * (COLS // slots), axis=1)

    lane = lax.broadcasted_iota(jnp.int32, (rows, COLS), 1)
    parity = lax.broadcasted_iota(jnp.int32, (rows, COLS), 0) % 2
    slot = lane % slots
    mine = (lane // slots) == parity
    columns = spread_lanes(columns_ref[...])
    live = mine & (slot < count_ref[...])
    offset = (columns.astype(jnp.float32) - 0.5 * (COLS - 1)) / radius_ref[...].astype(jnp.float32)
    weight = 1.0 / (1.0 + offset * offset) / spread_lanes(variance_ref[...])
    column_lanes[...] = jnp.where(mine, columns, -1)
    weight_lanes[...] = jnp.where(live, weight, 0.0)
    value_lanes[...] = jnp.where(mine, spread_lanes(value_ref[...]), 0.0)

    neighbours = (band > 0).astype(jnp.int32) + (band < bands - 1).astype(jnp.int32)
    pl.semaphore_wait(barrier, devices - 1 + neighbours)

    def halo(side):
        source, target, other = (
            (pl.ds(rows - EDGE, EDGE), pl.ds(0, EDGE), band + 1)
            if side == 0
            else (pl.ds(0, EDGE), pl.ds(EDGE + rows, EDGE), band - 1)
        )
        return [
            pltpu.make_async_remote_copy(
                src_ref=ref.at[:, source, :],
                dst_ref=extended.at[place, target, body],
                send_sem=halo_send.at[side, n],
                recv_sem=halo_recv.at[side, n],
                device_id={"tile": other},
            )
            for n, (ref, place) in enumerate(
                ((ensemble, pl.ds(0, local)), (velocity, pl.ds(local, 2)))
            )
        ]

    has = (band < bands - 1, band > 0)
    for side in range(2):

        @pl.when(has[side])
        def _():
            for copy in halo(side):
                copy.start()

    for load in loads:
        load.wait()

    window = step + 2 * EDGE
    reach = STRIP + 2 * COLS

    def forecast(c):
        first = pl.multiple_of(c * step, 8)

        @pl.loop(0, width // STRIP)
        def _(strip):
            lanes = pl.ds(pl.multiple_of(strip * STRIP, COLS), reach)
            span = pl.ds(first, window)
            u = extended[local, span, lanes]
            v = extended[local + 1, span, lanes]

            def nxt(x, axis):
                return pltpu.roll(x, x.shape[axis] - 1, axis)

            def prv(x, axis):
                return pltpu.roll(x, 1, axis)

            a = 0.5 * (u + nxt(u, 0))
            b = 0.5 * (v + nxt(v, 1))
            before_a, before_b = prv(a, 0), prv(b, 1)
            low_a, high_a = jnp.minimum(a, 0.0), jnp.maximum(before_a, 0.0)
            low_b, high_b = jnp.minimum(b, 0.0), jnp.maximum(before_b, 0.0)
            centre = (
                1.0
                - (jnp.maximum(a, 0.0) - jnp.minimum(before_a, 0.0))
                - (jnp.maximum(b, 0.0) - jnp.minimum(before_b, 0.0))
            )
            row = band * rows + c * step - EDGE + lax.broadcasted_iota(jnp.int32, u.shape, 0)
            col = strip * STRIP - COLS + lax.broadcasted_iota(jnp.int32, u.shape, 1)
            inside = (row >= 0) & (row < rows * bands) & (col >= 0) & (col < width)

            def substep(f):
                return (
                    centre * f
                    + (high_a * prv(f, 0) - low_a * nxt(f, 0))
                    + (high_b * prv(f, 1) - low_b * nxt(f, 1))
                )

            for m in range(local):
                f = extended[m, span, lanes]
                f = substep(jnp.where(inside, substep(f), 0.0))
                for h in range(STRIP // COLS):
                    outgoing[c, strip * (STRIP // COLS) + h, pl.ds(m * step, step), :] = f[
                        EDGE : EDGE + step, COLS * (1 + h) : COLS * (2 + h)
                    ]

        own = pltpu.make_async_copy(
            outgoing.at[c, me], gathered.at[c, pl.ds(me * part, part)], there_own.at[c]
        )
        own.start()

        @pl.loop(1, devices)
        def _(k):
            peer = lax.rem(me + k, devices)
            pltpu.make_async_remote_copy(
                src_ref=outgoing.at[c, peer],
                dst_ref=gathered.at[c, pl.ds(me * part, part)],
                send_sem=there_send.at[c],
                recv_sem=there_recv.at[c],
                device_id={"member": peer},
            ).start()

    @pl.loop(1, chunks - 1)
    def _(c):
        forecast(c)

    for side in range(2):

        @pl.when(has[1 - side])
        def _():
            for copy in halo(side):
                copy.wait_recv()

    @pl.loop(0, 2)
    def _(k):
        forecast(k * (chunks - 1))

    two = 2 * members
    row_index = lax.broadcasted_iota(jnp.int32, (two, two), 0)
    col_index = lax.broadcasted_iota(jnp.int32, (two, two), 1)
    identity = (row_index == col_index).astype(jnp.float32)
    upper = lax.broadcasted_iota(jnp.int32, (two, 1), 0) < members
    sublane = lax.broadcasted_iota(jnp.int32, (COLS, COLS), 0)
    across = (((1,), (1,)), ((), ()))

    def analyse(c, base):
        pairs = []
        for n in range(PAIRS):
            halves, seen, means, weight, value, averages = [], [], [], 0.0, 0.0, []
            for h in range(2):
                r = base + 2 * n + h
                tile_row = c * step + r
                x = gathered[c, pl.ds(r, members, stride=step), :]
                average = jnp.sum(x, axis=0, keepdims=True) * (1.0 / members)
                anomaly = x - average
                hit = (column_lanes[pl.ds(tile_row, 1), :] == sublane).astype(jnp.float32)
                hit = hit.astype(jnp.bfloat16)
                both = jnp.concatenate(
                    [anomaly, jnp.broadcast_to(average, (8, COLS))], axis=0
                )
                high, low = split(both)
                picked = jnp.dot(high, hit, preferred_element_type=jnp.float32) + jnp.dot(
                    low, hit, preferred_element_type=jnp.float32
                )
                halves.append(anomaly)
                averages.append(average)
                seen.append(picked[0:members])
                means.append(picked[members : members + 1])
                weight = weight + weight_lanes[pl.ds(tile_row, 1), :]
                value = value + value_lanes[pl.ds(tile_row, 1), :]
            spread = jnp.concatenate(seen, axis=0)
            scaled = spread * weight
            projected = jnp.sum(
                scaled * (value - (means[0] + means[1])), axis=1, keepdims=True
            )
            pairs.append((halves, averages, spread, scaled, projected))

        systems = [
            product(split(scaled), split(spread), across) + (members - 1.0) * identity
            for _, _, spread, scaled, _ in pairs
        ]
        norms = []
        for system in systems:
            squares = jnp.sum(system * system, axis=1, keepdims=True)
            norms.append(
                jnp.sqrt(
                    jnp.where(
                        upper,
                        jnp.sum(squares[0:members], axis=0, keepdims=True),
                        jnp.sum(squares[members:], axis=0, keepdims=True),
                    )
                )
            )
        roots = [system / norm for system, norm in zip(systems, norms)]
        inverses = [None] * PAIRS
        for sweep in range(SWEEPS):
            if sweep == 0:
                factors = [1.5 * identity - 0.5 * root for root in roots]
                inverses = factors
                parts = [split(factor) for factor in factors]
                inverse_parts = parts
                root_parts = [split(root) for root in roots]
            else:
                factors = [
                    1.5 * identity - 0.5 * product(z, y)
                    for z, y in zip(inverse_parts, root_parts)
                ]
                parts = [split(factor) for factor in factors]
                inverses = [product(p, z) for p, z in zip(parts, inverse_parts)]
                inverse_parts = [split(z) for z in inverses]
            if sweep < SWEEPS - 1:
                roots = [product(y, p) for y, p in zip(root_parts, parts)]
                root_parts = [split(y) for y in roots]
        for n in range(PAIRS):
            halves, averages, _, _, projected = pairs[n]
            inverse = inverses[n] * lax.rsqrt(norms[n])
            halfway = jnp.sum(inverse * projected, axis=0, keepdims=True)
            mean_weight = jnp.sum(inverse * halfway, axis=1, keepdims=True)
            anomaly = jnp.concatenate(halves, axis=0)
            moved = product(split(math.sqrt(members - 1.0) * inverse), split(anomaly))
            shift = mean_weight * anomaly
            for h in range(2):
                inner = slice(h * members, (h + 1) * members)
                centre = averages[h] + jnp.sum(shift[inner], axis=0, keepdims=True)
                analysed[c, pl.ds(base + 2 * n + h, members, stride=step), :] = (
                    moved[inner] + centre
                )

    def back(c, peer):
        return [
            pltpu.make_async_remote_copy(
                src_ref=analysed.at[c, pl.ds(peer * part + m * step, step)],
                dst_ref=out.at[
                    m,
                    pl.ds(pl.multiple_of(c * step, 8), step),
                    pl.ds(pl.multiple_of(me * COLS, COLS), COLS),
                ],
                send_sem=back_send.at[c],
                recv_sem=back_recv.at[c],
                device_id={"member": peer},
            )
            for m in range(local)
        ]

    def keep(c):
        return [
            pltpu.make_async_copy(
                analysed.at[c, pl.ds(me * part + m * step, step)],
                out.at[
                    m,
                    pl.ds(pl.multiple_of(c * step, 8), step),
                    pl.ds(pl.multiple_of(me * COLS, COLS), COLS),
                ],
                back_own.at[c, m],
            )
            for m in range(local)
        ]

    others = (devices - 1) * part

    def whole(ref, c, sem):
        piece = ref.at[c, pl.ds(0, others)]
        return pltpu.make_async_copy(piece, piece, sem.at[c])

    @pl.loop(0, chunks)
    def _(k):
        c = jnp.where(
            k < chunks - 2, k + 1, (k - (chunks - 2)) * (chunks - 1)
        )
        pltpu.make_async_copy(
            outgoing.at[c, me], gathered.at[c, pl.ds(me * part, part)], there_own.at[c]
        ).wait()
        whole(gathered, c, there_recv).wait()

        @pl.loop(0, step // (2 * PAIRS))
        def _(group):
            analyse(c, group * 2 * PAIRS)

        for copy in keep(c):
            copy.start()

        @pl.loop(1, devices)
        def _(j):
            for copy in back(c, lax.rem(me + j, devices)):
                copy.start()

    for side in range(2):

        @pl.when(has[side])
        def _():
            for copy in halo(side):
                copy.wait_send()

    @pl.loop(0, chunks)
    def _(c):
        whole(gathered, c, there_send).wait()
        whole(analysed, c, back_send).wait()
        for copy in keep(c):
            copy.wait()
        landed = out.at[
            :, pl.ds(pl.multiple_of(c * step, 8), step), pl.ds(0, (devices - 1) * COLS)
        ]
        pltpu.make_async_copy(landed, landed, back_recv.at[c]).wait()


def per_device(
    ensemble,
    velocity,
    observed_column,
    observation_slot_count,
    local_radius,
    observed_value,
    error_variance,
):
    devices, bands = lax.axis_size("member"), lax.axis_size("tile")
    local, rows, width = ensemble.shape
    slots = observed_column.shape[2]
    step = ROWS_PER_CHUNK
    chunks = rows // step
    part = local * step
    members = devices * local
    sizes = (devices, bands, local, rows, width, step, slots)
    vmem = pl.BlockSpec(memory_space=pltpu.VMEM)
    anywhere = pl.BlockSpec(memory_space=pl.ANY)
    dma = pltpu.SemaphoreType.DMA
    return pl.pallas_call(
        functools.partial(kernel, sizes),
        out_shape=jax.ShapeDtypeStruct(ensemble.shape, jnp.float32),
        in_specs=[anywhere] * 2 + [vmem] * 5,
        out_specs=anywhere,
        scratch_shapes=[
            pltpu.VMEM((local + 2, rows + 2 * EDGE, width + 2 * COLS), jnp.float32),
            pltpu.VMEM((chunks, devices, part, COLS), jnp.float32),
            pltpu.VMEM((chunks, members * step, COLS), jnp.float32),
            pltpu.VMEM((chunks, members * step, COLS), jnp.float32),
            pltpu.VMEM((rows, COLS), jnp.int32),
            pltpu.VMEM((rows, COLS), jnp.float32),
            pltpu.VMEM((rows, COLS), jnp.float32),
            dma((2,)),
            dma((2, 2)),
            dma((2, 2)),
            dma((chunks,)),
            dma((chunks,)),
            dma((chunks,)),
            dma((chunks,)),
            dma((chunks,)),
            dma((chunks, local)),
        ],
        compiler_params=pltpu.CompilerParams(
            collective_id=0, has_side_effects=True, vmem_limit_bytes=48 * 1024 * 1024
        ),
    )(
        ensemble,
        velocity,
        observed_column.reshape(rows, slots),
        observation_slot_count,
        local_radius,
        observed_value.reshape(rows, slots),
        error_variance.reshape(rows, slots),
    )


def solution(mesh):
    placed = (
        P("member", "tile", None),
        P(None, "tile", None),
        P("tile", "member", None),
        P("tile", "member"),
        P("tile", "member"),
        P("tile", "member", None),
        P("tile", "member", None),
    )
    return jax.shard_map(
        per_device, mesh=mesh, in_specs=placed, out_specs=P("member", "tile", None), check_vma=False
    )
```

```python
import functools
import math

import jax
import jax.numpy as jnp
from jax import lax
from jax.experimental import pallas as pl
from jax.experimental.pallas import tpu as pltpu
from jax.sharding import PartitionSpec as P

COLS = 128
SWEEPS = 6
EDGE = 8
STRIP = 256
ROWS_PER_CHUNK = 16
PAIRS = 4


def split(x):
    high = x.astype(jnp.bfloat16)
    low = (x - high.astype(jnp.float32)).astype(jnp.bfloat16)
    return high, low


def product(a, b, dims=(((1,), (0,)), ((), ()))):
    dot = functools.partial(
        lax.dot_general, dimension_numbers=dims, preferred_element_type=jnp.float32
    )
    return dot(a[0], b[0]) + (dot(a[0], b[1]) + dot(a[1], b[0]))


def kernel(
    sizes,
    ensemble,
    velocity,
    columns_ref,
    count_ref,
    radius_ref,
    value_ref,
    variance_ref,
    out,
    extended,
    outgoing,
    gathered,
    analysed,
    column_lanes,
    weight_lanes,
    value_lanes,
    load_sem,
    halo_send,
    halo_recv,
    there_send,
    there_recv,
    there_own,
    back_send,
    back_recv,
    back_own,
):
    devices, bands, local, rows, width, step, slots = sizes
    members = devices * local
    chunks = rows // step
    me = lax.axis_index("member")
    band = lax.axis_index("tile")
    part = local * step
    body = pl.ds(COLS, width)

    loads = [
        pltpu.make_async_copy(
            ensemble, extended.at[pl.ds(0, local), pl.ds(EDGE, rows), body], load_sem.at[0]
        ),
        pltpu.make_async_copy(
            velocity, extended.at[pl.ds(local, 2), pl.ds(EDGE, rows), body], load_sem.at[1]
        ),
    ]
    for load in loads:
        load.start()

    barrier = pltpu.get_barrier_semaphore()

    @pl.loop(1, devices)
    def _(k):
        pl.semaphore_signal(barrier, inc=1, device_id={"member": lax.rem(me + k, devices)})

    @pl.when(band > 0)
    def _():
        pl.semaphore_signal(barrier, inc=1, device_id={"tile": band - 1})

    @pl.when(band < bands - 1)
    def _():
        pl.semaphore_signal(barrier, inc=1, device_id={"tile": band + 1})

    extended[:, :, 0:COLS] = jnp.zeros((local + 2, rows + 2 * EDGE, COLS), jnp.float32)
    extended[:, :, COLS + width :] = jnp.zeros((local + 2, rows + 2 * EDGE, COLS), jnp.float32)

    @pl.when(band == 0)
    def _():
        extended[:, 0:EDGE, COLS : COLS + width] = jnp.zeros((local + 2, EDGE, width), jnp.float32)

    @pl.when(band == bands - 1)
    def _():
        extended[:, EDGE + rows :, COLS : COLS + width] = jnp.zeros(
            (local + 2, EDGE, width), jnp.float32
        )

    neighbours = (band > 0).astype(jnp.int32) + (band < bands - 1).astype(jnp.int32)
    pl.semaphore_wait(barrier, devices - 1 + neighbours)

    def halo(side):
        source, target, other = (
            (pl.ds(rows - EDGE, EDGE), pl.ds(0, EDGE), band + 1)
            if side == 0
            else (pl.ds(0, EDGE), pl.ds(EDGE + rows, EDGE), band - 1)
        )
        return [
            pltpu.make_async_remote_copy(
                src_ref=ref.at[:, source, :],
                dst_ref=extended.at[place, target, body],
                send_sem=halo_send.at[side, n],
                recv_sem=halo_recv.at[side, n],
                device_id={"tile": other},
            )
            for n, (ref, place) in enumerate(
                ((ensemble, pl.ds(0, local)), (velocity, pl.ds(local, 2)))
            )
        ]

    has = (band < bands - 1, band > 0)
    for side in range(2):

        @pl.when(has[side])
        def _():
            for copy in halo(side):
                copy.start()

    for load in loads:
        load.wait()

    def far_first(n, place, count):
        half = count // 2
        near_base = (place // half) * half
        base = jnp.where(n < half, half - near_base, near_base)
        return base + lax.rem(place + n, half)

    per_strip = STRIP // COLS
    strips = width // STRIP
    window = step + 2 * EDGE
    reach = STRIP + 2 * COLS

    def forecast(c):
        first = pl.multiple_of(c * step, 8)

        @pl.loop(0, strips)
        def _(turn):
            strip = far_first(turn, me // per_strip, strips)
            lanes = pl.ds(pl.multiple_of(strip * STRIP, COLS), reach)
            span = pl.ds(first, window)
            u = extended[local, span, lanes]
            v = extended[local + 1, span, lanes]

            def nxt(x, axis):
                return pltpu.roll(x, x.shape[axis] - 1, axis)

            def prv(x, axis):
                return pltpu.roll(x, 1, axis)

            a = 0.5 * (u + nxt(u, 0))
            b = 0.5 * (v + nxt(v, 1))
            before_a, before_b = prv(a, 0), prv(b, 1)
            low_a, high_a = jnp.minimum(a, 0.0), jnp.maximum(before_a, 0.0)
            low_b, high_b = jnp.minimum(b, 0.0), jnp.maximum(before_b, 0.0)
            centre = (
                1.0
                - (jnp.maximum(a, 0.0) - jnp.minimum(before_a, 0.0))
                - (jnp.maximum(b, 0.0) - jnp.minimum(before_b, 0.0))
            )
            row = band * rows + c * step - EDGE + lax.broadcasted_iota(jnp.int32, u.shape, 0)
            col = strip * STRIP - COLS + lax.broadcasted_iota(jnp.int32, u.shape, 1)
            inside = (row >= 0) & (row < rows * bands) & (col >= 0) & (col < width)

            def substep(f):
                return (
                    centre * f
                    + (high_a * prv(f, 0) - low_a * nxt(f, 0))
                    + (high_b * prv(f, 1) - low_b * nxt(f, 1))
                )

            for m in range(local):
                f = extended[m, span, lanes]
                f = substep(jnp.where(inside, substep(f), 0.0))
                for h in range(per_strip):
                    outgoing[c, strip * per_strip + h, pl.ds(m * step, step), :] = f[
                        EDGE : EDGE + step, COLS * (1 + h) : COLS * (2 + h)
                    ]

            for h in range(per_strip):
                peer = strip * per_strip + h

                @pl.when(peer == me)
                def _():
                    pltpu.make_async_copy(
                        outgoing.at[c, me], gathered.at[c, pl.ds(me * part, part)], there_own.at[c]
                    ).start()

                @pl.when(peer != me)
                def _():
                    pltpu.make_async_remote_copy(
                        src_ref=outgoing.at[c, peer],
                        dst_ref=gathered.at[c, pl.ds(me * part, part)],
                        send_sem=there_send.at[c],
                        recv_sem=there_recv.at[c],
                        device_id={"member": peer},
                    ).start()

    @pl.loop(1, chunks - 1)
    def _(c):
        forecast(c)

    for side in range(2):

        @pl.when(has[1 - side])
        def _():
            for copy in halo(side):
                copy.wait_recv()

    @pl.loop(0, 2)
    def _(k):
        forecast(k * (chunks - 1))

    def spread_lanes(x):
        return jnp.concatenate([x] * (COLS // slots), axis=1)

    lane = lax.broadcasted_iota(jnp.int32, (rows, COLS), 1)
    parity = lax.broadcasted_iota(jnp.int32, (rows, COLS), 0) % 2
    slot = lane % slots
    mine = (lane // slots) == parity
    columns = spread_lanes(columns_ref[...].T)
    square = (rows, rows)
    diagonal = lax.broadcasted_iota(jnp.int32, square, 0) == lax.broadcasted_iota(
        jnp.int32, square, 1
    )

    def upright(ref):
        line = jnp.broadcast_to(ref[...].astype(jnp.float32), square)
        return jnp.sum(jnp.where(diagonal, line, 0.0), axis=1, keepdims=True)

    live = mine & (slot.astype(jnp.float32) < upright(count_ref))
    offset = (columns.astype(jnp.float32) - 0.5 * (COLS - 1)) / upright(radius_ref)
    weight = 1.0 / (1.0 + offset * offset) / spread_lanes(variance_ref[...].T)
    column_lanes[...] = jnp.where(mine, columns, -1)
    weight_lanes[...] = jnp.where(live, weight, 0.0)
    value_lanes[...] = jnp.where(mine, spread_lanes(value_ref[...].T), 0.0)

    two = 2 * members
    row_index = lax.broadcasted_iota(jnp.int32, (two, two), 0)
    col_index = lax.broadcasted_iota(jnp.int32, (two, two), 1)
    identity = (row_index == col_index).astype(jnp.float32)
    upper = lax.broadcasted_iota(jnp.int32, (two, 1), 0) < members
    sublane = lax.broadcasted_iota(jnp.int32, (COLS, COLS), 0)
    across = (((1,), (1,)), ((), ()))

    def analyse(c, base):
        pairs = []
        for n in range(PAIRS):
            halves, seen, means, weight, value, averages = [], [], [], 0.0, 0.0, []
            for h in range(2):
                r = base + 2 * n + h
                tile_row = c * step + r
                x = gathered[c, pl.ds(r, members, stride=step), :]
                average = jnp.sum(x, axis=0, keepdims=True) * (1.0 / members)
                anomaly = x - average
                hit = (column_lanes[pl.ds(tile_row, 1), :] == sublane).astype(jnp.float32)
                hit = hit.astype(jnp.bfloat16)
                both = jnp.concatenate(
                    [anomaly, jnp.broadcast_to(average, (8, COLS))], axis=0
                )
                high, low = split(both)
                picked = jnp.dot(high, hit, preferred_element_type=jnp.float32) + jnp.dot(
                    low, hit, preferred_element_type=jnp.float32
                )
                halves.append(anomaly)
                averages.append(average)
                seen.append(picked[0:members])
                means.append(picked[members : members + 1])
                weight = weight + weight_lanes[pl.ds(tile_row, 1), :]
                value = value + value_lanes[pl.ds(tile_row, 1), :]
            spread = jnp.concatenate(seen, axis=0)
            scaled = spread * weight
            projected = jnp.sum(
                scaled * (value - (means[0] + means[1])), axis=1, keepdims=True
            )
            pairs.append((halves, averages, spread, scaled, projected))

        systems = [
            product(split(scaled), split(spread), across) + (members - 1.0) * identity
            for _, _, spread, scaled, _ in pairs
        ]
        norms = []
        for system in systems:
            squares = jnp.sum(system * system, axis=1, keepdims=True)
            norms.append(
                jnp.sqrt(
                    jnp.where(
                        upper,
                        jnp.sum(squares[0:members], axis=0, keepdims=True),
                        jnp.sum(squares[members:], axis=0, keepdims=True),
                    )
                )
            )
        roots = [system / norm for system, norm in zip(systems, norms)]
        inverses = [None] * PAIRS
        for sweep in range(SWEEPS):
            if sweep == 0:
                factors = [1.5 * identity - 0.5 * root for root in roots]
                inverses = factors
                parts = [split(factor) for factor in factors]
                inverse_parts = parts
                root_parts = [split(root) for root in roots]
            else:
                factors = [
                    1.5 * identity - 0.5 * product(z, y)
                    for z, y in zip(inverse_parts, root_parts)
                ]
                parts = [split(factor) for factor in factors]
                inverses = [product(p, z) for p, z in zip(parts, inverse_parts)]
                inverse_parts = [split(z) for z in inverses]
            if sweep < SWEEPS - 1:
                roots = [product(y, p) for y, p in zip(root_parts, parts)]
                root_parts = [split(y) for y in roots]
        for n in range(PAIRS):
            halves, averages, _, _, projected = pairs[n]
            inverse = inverses[n] * lax.rsqrt(norms[n])
            halfway = jnp.sum(inverse * projected, axis=0, keepdims=True)
            mean_weight = jnp.sum(inverse * halfway, axis=1, keepdims=True)
            anomaly = jnp.concatenate(halves, axis=0)
            moved = product(split(math.sqrt(members - 1.0) * inverse), split(anomaly))
            shift = mean_weight * anomaly
            for h in range(2):
                inner = slice(h * members, (h + 1) * members)
                centre = averages[h] + jnp.sum(shift[inner], axis=0, keepdims=True)
                analysed[c, pl.ds(base + 2 * n + h, members, stride=step), :] = (
                    moved[inner] + centre
                )

    def back(c, peer):
        return [
            pltpu.make_async_remote_copy(
                src_ref=analysed.at[c, pl.ds(peer * part + m * step, step)],
                dst_ref=out.at[
                    m,
                    pl.ds(pl.multiple_of(c * step, 8), step),
                    pl.ds(pl.multiple_of(me * COLS, COLS), COLS),
                ],
                send_sem=back_send.at[c],
                recv_sem=back_recv.at[c],
                device_id={"member": peer},
            )
            for m in range(local)
        ]

    def keep(c):
        return [
            pltpu.make_async_copy(
                analysed.at[c, pl.ds(me * part + m * step, step)],
                out.at[
                    m,
                    pl.ds(pl.multiple_of(c * step, 8), step),
                    pl.ds(pl.multiple_of(me * COLS, COLS), COLS),
                ],
                back_own.at[c, m],
            )
            for m in range(local)
        ]

    others = (devices - 1) * part

    def whole(ref, c, sem):
        piece = ref.at[c, pl.ds(0, others)]
        return pltpu.make_async_copy(piece, piece, sem.at[c])

    @pl.loop(0, chunks)
    def _(k):
        c = jnp.where(
            k < chunks - 2, k + 1, (k - (chunks - 2)) * (chunks - 1)
        )
        pltpu.make_async_copy(
            outgoing.at[c, me], gathered.at[c, pl.ds(me * part, part)], there_own.at[c]
        ).wait()
        whole(gathered, c, there_recv).wait()

        @pl.loop(0, step // (2 * PAIRS))
        def _(group):
            analyse(c, group * 2 * PAIRS)

        for copy in keep(c):
            copy.start()

        @pl.loop(0, devices)
        def _(turn):
            peer = far_first(turn, me, devices)

            @pl.when(peer != me)
            def _():
                for copy in back(c, peer):
                    copy.start()

    for side in range(2):

        @pl.when(has[side])
        def _():
            for copy in halo(side):
                copy.wait_send()

    @pl.loop(0, chunks)
    def _(c):
        whole(gathered, c, there_send).wait()
        whole(analysed, c, back_send).wait()
        for copy in keep(c):
            copy.wait()
        landed = out.at[
            :, pl.ds(pl.multiple_of(c * step, 8), step), pl.ds(0, (devices - 1) * COLS)
        ]
        pltpu.make_async_copy(landed, landed, back_recv.at[c]).wait()


def per_device(
    ensemble,
    velocity,
    observed_column,
    observation_slot_count,
    local_radius,
    observed_value,
    error_variance,
):
    devices, bands = lax.axis_size("member"), lax.axis_size("tile")
    local, rows, width = ensemble.shape
    slots = observed_column.shape[2]
    step = ROWS_PER_CHUNK
    chunks = rows // step
    part = local * step
    members = devices * local
    sizes = (devices, bands, local, rows, width, step, slots)
    vmem = pl.BlockSpec(memory_space=pltpu.VMEM)
    anywhere = pl.BlockSpec(memory_space=pl.ANY)
    dma = pltpu.SemaphoreType.DMA
    return pl.pallas_call(
        functools.partial(kernel, sizes),
        out_shape=jax.ShapeDtypeStruct(ensemble.shape, jnp.float32),
        in_specs=[anywhere] * 2 + [vmem] * 5,
        out_specs=anywhere,
        scratch_shapes=[
            pltpu.VMEM((local + 2, rows + 2 * EDGE, width + 2 * COLS), jnp.float32),
            pltpu.VMEM((chunks, devices, part, COLS), jnp.float32),
            pltpu.VMEM((chunks, members * step, COLS), jnp.float32),
            pltpu.VMEM((chunks, members * step, COLS), jnp.float32),
            pltpu.VMEM((rows, COLS), jnp.int32),
            pltpu.VMEM((rows, COLS), jnp.float32),
            pltpu.VMEM((rows, COLS), jnp.float32),
            dma((2,)),
            dma((2, 2)),
            dma((2, 2)),
            dma((chunks,)),
            dma((chunks,)),
            dma((chunks,)),
            dma((chunks,)),
            dma((chunks,)),
            dma((chunks, local)),
        ],
        compiler_params=pltpu.CompilerParams(
            collective_id=0, has_side_effects=True, vmem_limit_bytes=62 * 1024 * 1024
        ),
    )(
        ensemble,
        velocity,
        observed_column.reshape(rows, slots).T,
        observation_slot_count.reshape(1, rows),
        local_radius.reshape(1, rows),
        observed_value.reshape(rows, slots).T,
        error_variance.reshape(rows, slots).T,
    )


def solution(mesh):
    placed = (
        P("member", "tile", None),
        P(None, "tile", None),
        P("tile", "member", None),
        P("tile", "member"),
        P("tile", "member"),
        P("tile", "member", None),
        P("tile", "member", None),
    )
    return jax.shard_map(
        per_device, mesh=mesh, in_specs=placed, out_specs=P("member", "tile", None), check_vma=False
    )
```

```python
import functools
import math

import jax
import jax.numpy as jnp
from jax import lax
from jax.experimental import pallas as pl
from jax.experimental.pallas import tpu as pltpu
from jax.sharding import PartitionSpec as P

COLS = 128
SWEEPS = 6
EDGE = 8
STRIP = 256
ROWS_PER_CHUNK = 16
PAIRS = 4


def split(x):
    high = x.astype(jnp.bfloat16)
    low = (x - high.astype(jnp.float32)).astype(jnp.bfloat16)
    return high, low


def product(a, b, dims=(((1,), (0,)), ((), ()))):
    dot = functools.partial(
        lax.dot_general, dimension_numbers=dims, preferred_element_type=jnp.float32
    )
    return dot(a[0], b[0]) + (dot(a[0], b[1]) + dot(a[1], b[0]))


def kernel(
    sizes,
    ensemble,
    velocity,
    columns_ref,
    count_ref,
    radius_ref,
    value_ref,
    variance_ref,
    out,
    extended,
    outgoing,
    gathered,
    analysed,
    column_lanes,
    weight_lanes,
    value_lanes,
    load_sem,
    halo_send,
    halo_recv,
    there_send,
    there_recv,
    there_own,
    back_send,
    back_recv,
    back_own,
):
    devices, bands, local, rows, width, step, slots = sizes
    members = devices * local
    chunks = rows // step
    me = lax.axis_index("member")
    band = lax.axis_index("tile")
    part = local * step
    body = pl.ds(COLS, width)

    loads = [
        pltpu.make_async_copy(
            ensemble, extended.at[pl.ds(0, local), pl.ds(EDGE, rows), body], load_sem.at[0]
        ),
        pltpu.make_async_copy(
            velocity, extended.at[pl.ds(local, 2), pl.ds(EDGE, rows), body], load_sem.at[1]
        ),
    ]
    for load in loads:
        load.start()

    barrier = pltpu.get_barrier_semaphore()

    @pl.loop(1, devices)
    def _(k):
        pl.semaphore_signal(barrier, inc=1, device_id={"member": lax.rem(me + k, devices)})

    @pl.when(band > 0)
    def _():
        pl.semaphore_signal(barrier, inc=1, device_id={"tile": band - 1})

    @pl.when(band < bands - 1)
    def _():
        pl.semaphore_signal(barrier, inc=1, device_id={"tile": band + 1})

    extended[:, :, 0:COLS] = jnp.zeros((local + 2, rows + 2 * EDGE, COLS), jnp.float32)
    extended[:, :, COLS + width :] = jnp.zeros((local + 2, rows + 2 * EDGE, COLS), jnp.float32)

    @pl.when(band == 0)
    def _():
        extended[:, 0:EDGE, COLS : COLS + width] = jnp.zeros((local + 2, EDGE, width), jnp.float32)

    @pl.when(band == bands - 1)
    def _():
        extended[:, EDGE + rows :, COLS : COLS + width] = jnp.zeros(
            (local + 2, EDGE, width), jnp.float32
        )

    neighbours = (band > 0).astype(jnp.int32) + (band < bands - 1).astype(jnp.int32)
    pl.semaphore_wait(barrier, devices - 1 + neighbours)

    def halo(side):
        source, target, other = (
            (pl.ds(rows - EDGE, EDGE), pl.ds(0, EDGE), band + 1)
            if side == 0
            else (pl.ds(0, EDGE), pl.ds(EDGE + rows, EDGE), band - 1)
        )
        return [
            pltpu.make_async_remote_copy(
                src_ref=ref.at[:, source, :],
                dst_ref=extended.at[place, target, body],
                send_sem=halo_send.at[side, n],
                recv_sem=halo_recv.at[side, n],
                device_id={"tile": other},
            )
            for n, (ref, place) in enumerate(
                ((ensemble, pl.ds(0, local)), (velocity, pl.ds(local, 2)))
            )
        ]

    has = (band < bands - 1, band > 0)
    for side in range(2):

        @pl.when(has[side])
        def _():
            for copy in halo(side):
                copy.start()

    for load in loads:
        load.wait()

    def far_first(n, place, count):
        half = count // 2
        near_base = (place // half) * half
        base = jnp.where(n < half, half - near_base, near_base)
        return base + lax.rem(place + n, half)

    per_strip = STRIP // COLS
    strips = width // STRIP
    window = step + 2 * EDGE
    reach = STRIP + 2 * COLS

    def forecast(c):
        first = pl.multiple_of(c * step, 8)

        @pl.loop(0, strips)
        def _(turn):
            strip = far_first(turn, me // per_strip, strips)
            lanes = pl.ds(pl.multiple_of(strip * STRIP, COLS), reach)
            span = pl.ds(first, window)
            u = extended[local, span, lanes]
            v = extended[local + 1, span, lanes]

            def nxt(x, axis):
                return pltpu.roll(x, x.shape[axis] - 1, axis)

            def prv(x, axis):
                return pltpu.roll(x, 1, axis)

            a = 0.5 * (u + nxt(u, 0))
            b = 0.5 * (v + nxt(v, 1))
            before_a, before_b = prv(a, 0), prv(b, 1)
            low_a, high_a = jnp.minimum(a, 0.0), jnp.maximum(before_a, 0.0)
            low_b, high_b = jnp.minimum(b, 0.0), jnp.maximum(before_b, 0.0)
            centre = (
                1.0
                - (jnp.maximum(a, 0.0) - jnp.minimum(before_a, 0.0))
                - (jnp.maximum(b, 0.0) - jnp.minimum(before_b, 0.0))
            )
            row = band * rows + c * step - EDGE + lax.broadcasted_iota(jnp.int32, u.shape, 0)
            col = strip * STRIP - COLS + lax.broadcasted_iota(jnp.int32, u.shape, 1)
            inside = (row >= 0) & (row < rows * bands) & (col >= 0) & (col < width)

            def substep(f):
                return (
                    centre * f
                    + (high_a * prv(f, 0) - low_a * nxt(f, 0))
                    + (high_b * prv(f, 1) - low_b * nxt(f, 1))
                )

            for m in range(local):
                f = extended[m, span, lanes]
                f = substep(jnp.where(inside, substep(f), 0.0))
                for h in range(per_strip):
                    outgoing[c, strip * per_strip + h, pl.ds(m * step, step), :] = f[
                        EDGE : EDGE + step, COLS * (1 + h) : COLS * (2 + h)
                    ]

            for h in range(per_strip):
                peer = strip * per_strip + h

                @pl.when(peer == me)
                def _():
                    pltpu.make_async_copy(
                        outgoing.at[c, me], gathered.at[c, pl.ds(me * part, part)], there_own.at[c]
                    ).start()

                @pl.when(peer != me)
                def _():
                    pltpu.make_async_remote_copy(
                        src_ref=outgoing.at[c, peer],
                        dst_ref=gathered.at[c, pl.ds(me * part, part)],
                        send_sem=there_send.at[c],
                        recv_sem=there_recv.at[c],
                        device_id={"member": peer},
                    ).start()

    @pl.loop(1, chunks - 1)
    def _(c):
        forecast(c)

    for side in range(2):

        @pl.when(has[1 - side])
        def _():
            for copy in halo(side):
                copy.wait_recv()

    @pl.loop(0, 2)
    def _(k):
        forecast(k * (chunks - 1))

    def spread_lanes(x):
        return jnp.concatenate([x] * (COLS // slots), axis=1)

    lane = lax.broadcasted_iota(jnp.int32, (rows, COLS), 1)
    parity = lax.broadcasted_iota(jnp.int32, (rows, COLS), 0) % 2
    slot = lane % slots
    mine = (lane // slots) == parity
    columns = spread_lanes(columns_ref[...].T)
    square = (rows, rows)
    diagonal = lax.broadcasted_iota(jnp.int32, square, 0) == lax.broadcasted_iota(
        jnp.int32, square, 1
    )

    def upright(ref):
        line = jnp.broadcast_to(ref[...].astype(jnp.float32), square)
        return jnp.sum(jnp.where(diagonal, line, 0.0), axis=1, keepdims=True)

    live = mine & (slot.astype(jnp.float32) < upright(count_ref))
    offset = (columns.astype(jnp.float32) - 0.5 * (COLS - 1)) / upright(radius_ref)
    weight = 1.0 / (1.0 + offset * offset) / spread_lanes(variance_ref[...].T)
    column_lanes[...] = jnp.where(mine, columns, -1)
    weight_lanes[...] = jnp.where(live, weight, 0.0)
    value_lanes[...] = jnp.where(mine, spread_lanes(value_ref[...].T), 0.0)

    two = 2 * members
    row_index = lax.broadcasted_iota(jnp.int32, (two, two), 0)
    col_index = lax.broadcasted_iota(jnp.int32, (two, two), 1)
    identity = (row_index == col_index).astype(jnp.float32)
    upper = lax.broadcasted_iota(jnp.int32, (two, 1), 0) < members
    sublane = lax.broadcasted_iota(jnp.int32, (COLS, COLS), 0)
    across = (((1,), (1,)), ((), ()))

    def analyse(c, base):
        pairs = []
        for n in range(PAIRS):
            halves, seen, means, weight, value, averages = [], [], [], 0.0, 0.0, []
            for h in range(2):
                r = base + 2 * n + h
                tile_row = c * step + r
                x = gathered[c, pl.ds(r, members, stride=step), :]
                average = jnp.sum(x, axis=0, keepdims=True) * (1.0 / members)
                anomaly = x - average
                hit = (column_lanes[pl.ds(tile_row, 1), :] == sublane).astype(jnp.float32)
                hit = hit.astype(jnp.bfloat16)
                both = jnp.concatenate(
                    [anomaly, jnp.broadcast_to(average, (8, COLS))], axis=0
                )
                high, low = split(both)
                picked = jnp.dot(high, hit, preferred_element_type=jnp.float32) + jnp.dot(
                    low, hit, preferred_element_type=jnp.float32
                )
                halves.append(anomaly)
                averages.append(average)
                seen.append(picked[0:members])
                means.append(picked[members : members + 1])
                weight = weight + weight_lanes[pl.ds(tile_row, 1), :]
                value = value + value_lanes[pl.ds(tile_row, 1), :]
            spread = jnp.concatenate(seen, axis=0)
            scaled = spread * weight
            projected = jnp.sum(
                scaled * (value - (means[0] + means[1])), axis=1, keepdims=True
            )
            pairs.append((halves, averages, spread, scaled, projected))

        systems = [
            product(split(scaled), split(spread), across) + (members - 1.0) * identity
            for _, _, spread, scaled, _ in pairs
        ]
        norms = []
        for system in systems:
            squares = jnp.sum(system * system, axis=1, keepdims=True)
            norms.append(
                jnp.sqrt(
                    jnp.where(
                        upper,
                        jnp.sum(squares[0:members], axis=0, keepdims=True),
                        jnp.sum(squares[members:], axis=0, keepdims=True),
                    )
                )
            )
        roots = [system / norm for system, norm in zip(systems, norms)]
        inverses = [None] * PAIRS
        for sweep in range(SWEEPS):
            if sweep == 0:
                factors = [1.5 * identity - 0.5 * root for root in roots]
                inverses = factors
                parts = [split(factor) for factor in factors]
                inverse_parts = parts
                root_parts = [split(root) for root in roots]
            else:
                factors = [
                    1.5 * identity - 0.5 * product(z, y)
                    for z, y in zip(inverse_parts, root_parts)
                ]
                parts = [split(factor) for factor in factors]
                inverses = [product(p, z) for p, z in zip(parts, inverse_parts)]
                inverse_parts = [split(z) for z in inverses]
            if sweep < SWEEPS - 1:
                roots = [product(y, p) for y, p in zip(root_parts, parts)]
                root_parts = [split(y) for y in roots]
        for n in range(PAIRS):
            halves, averages, _, _, projected = pairs[n]
            inverse = inverses[n] * lax.rsqrt(norms[n])
            halfway = jnp.sum(inverse * projected, axis=0, keepdims=True)
            mean_weight = jnp.sum(inverse * halfway, axis=1, keepdims=True)
            anomaly = jnp.concatenate(halves, axis=0)
            moved = product(split(math.sqrt(members - 1.0) * inverse), split(anomaly))
            shift = mean_weight * anomaly
            for h in range(2):
                inner = slice(h * members, (h + 1) * members)
                centre = averages[h] + jnp.sum(shift[inner], axis=0, keepdims=True)
                analysed[c, pl.ds(base + 2 * n + h, members, stride=step), :] = (
                    moved[inner] + centre
                )

    group_rows = 2 * PAIRS

    def back(c, group, peer):
        return [
            pltpu.make_async_remote_copy(
                src_ref=analysed.at[
                    c,
                    pl.ds(
                        pl.multiple_of(peer * part + m * step + group * group_rows, 8),
                        group_rows,
                    ),
                ],
                dst_ref=out.at[
                    m,
                    pl.ds(pl.multiple_of(c * step + group * group_rows, 8), group_rows),
                    pl.ds(pl.multiple_of(me * COLS, COLS), COLS),
                ],
                send_sem=back_send.at[c],
                recv_sem=back_recv.at[c],
                device_id={"member": peer},
            )
            for m in range(local)
        ]

    def keep(c):
        return [
            pltpu.make_async_copy(
                analysed.at[c, pl.ds(me * part + m * step, step)],
                out.at[
                    m,
                    pl.ds(pl.multiple_of(c * step, 8), step),
                    pl.ds(pl.multiple_of(me * COLS, COLS), COLS),
                ],
                back_own.at[c, m],
            )
            for m in range(local)
        ]

    others = (devices - 1) * part

    def whole(ref, c, sem):
        piece = ref.at[c, pl.ds(0, others)]
        return pltpu.make_async_copy(piece, piece, sem.at[c])

    @pl.loop(0, chunks)
    def _(k):
        c = jnp.where(
            k < chunks - 2, k + 1, (k - (chunks - 2)) * (chunks - 1)
        )
        pltpu.make_async_copy(
            outgoing.at[c, me], gathered.at[c, pl.ds(me * part, part)], there_own.at[c]
        ).wait()
        whole(gathered, c, there_recv).wait()

        @pl.loop(0, step // group_rows)
        def _(group):
            analyse(c, group * group_rows)

            @pl.loop(0, devices)
            def _(turn):
                peer = far_first(turn, me, devices)

                @pl.when(peer != me)
                def _():
                    for copy in back(c, group, peer):
                        copy.start()

        for copy in keep(c):
            copy.start()

    for side in range(2):

        @pl.when(has[side])
        def _():
            for copy in halo(side):
                copy.wait_send()

    @pl.loop(0, chunks)
    def _(c):
        whole(gathered, c, there_send).wait()
        whole(analysed, c, back_send).wait()
        for copy in keep(c):
            copy.wait()
        landed = out.at[
            :, pl.ds(pl.multiple_of(c * step, 8), step), pl.ds(0, (devices - 1) * COLS)
        ]
        pltpu.make_async_copy(landed, landed, back_recv.at[c]).wait()


def per_device(
    ensemble,
    velocity,
    observed_column,
    observation_slot_count,
    local_radius,
    observed_value,
    error_variance,
):
    devices, bands = lax.axis_size("member"), lax.axis_size("tile")
    local, rows, width = ensemble.shape
    slots = observed_column.shape[2]
    step = ROWS_PER_CHUNK
    chunks = rows // step
    part = local * step
    members = devices * local
    sizes = (devices, bands, local, rows, width, step, slots)
    vmem = pl.BlockSpec(memory_space=pltpu.VMEM)
    anywhere = pl.BlockSpec(memory_space=pl.ANY)
    dma = pltpu.SemaphoreType.DMA
    return pl.pallas_call(
        functools.partial(kernel, sizes),
        out_shape=jax.ShapeDtypeStruct(ensemble.shape, jnp.float32),
        in_specs=[anywhere] * 2 + [vmem] * 5,
        out_specs=anywhere,
        scratch_shapes=[
            pltpu.VMEM((local + 2, rows + 2 * EDGE, width + 2 * COLS), jnp.float32),
            pltpu.VMEM((chunks, devices, part, COLS), jnp.float32),
            pltpu.VMEM((chunks, members * step, COLS), jnp.float32),
            pltpu.VMEM((chunks, members * step, COLS), jnp.float32),
            pltpu.VMEM((rows, COLS), jnp.int32),
            pltpu.VMEM((rows, COLS), jnp.float32),
            pltpu.VMEM((rows, COLS), jnp.float32),
            dma((2,)),
            dma((2, 2)),
            dma((2, 2)),
            dma((chunks,)),
            dma((chunks,)),
            dma((chunks,)),
            dma((chunks,)),
            dma((chunks,)),
            dma((chunks, local)),
        ],
        compiler_params=pltpu.CompilerParams(
            collective_id=0, has_side_effects=True, vmem_limit_bytes=62 * 1024 * 1024
        ),
    )(
        ensemble,
        velocity,
        observed_column.reshape(rows, slots).T,
        observation_slot_count.reshape(1, rows),
        local_radius.reshape(1, rows),
        observed_value.reshape(rows, slots).T,
        error_variance.reshape(rows, slots).T,
    )


def solution(mesh):
    placed = (
        P("member", "tile", None),
        P(None, "tile", None),
        P("tile", "member", None),
        P("tile", "member"),
        P("tile", "member"),
        P("tile", "member", None),
        P("tile", "member", None),
    )
    return jax.shard_map(
        per_device, mesh=mesh, in_specs=placed, out_specs=P("member", "tile", None), check_vma=False
    )
```

```python
import functools
import math

import jax
import jax.numpy as jnp
from jax import lax
from jax.experimental import pallas as pl
from jax.experimental.pallas import tpu as pltpu
from jax.sharding import PartitionSpec as P

COLS = 128
SWEEPS = 6
EDGE = 8
STRIP = 256
ROWS_PER_CHUNK = 16
PAIRS = 4


def split(x):
    high = x.astype(jnp.bfloat16)
    low = (x - high.astype(jnp.float32)).astype(jnp.bfloat16)
    return high, low


def product(a, b, dims=(((1,), (0,)), ((), ()))):
    dot = functools.partial(
        lax.dot_general, dimension_numbers=dims, preferred_element_type=jnp.float32
    )
    return dot(a[0], b[0]) + (dot(a[0], b[1]) + dot(a[1], b[0]))


def kernel(
    sizes,
    ensemble,
    velocity,
    columns_ref,
    count_ref,
    radius_ref,
    value_ref,
    variance_ref,
    out,
    extended,
    outgoing,
    gathered,
    analysed,
    column_lanes,
    weight_lanes,
    value_lanes,
    load_sem,
    halo_send,
    halo_recv,
    there_send,
    there_recv,
    there_own,
    back_send,
    back_recv,
    back_own,
):
    devices, bands, local, rows, width, step, slots = sizes
    members = devices * local
    chunks = rows // step
    me = lax.axis_index("member")
    band = lax.axis_index("tile")
    part = local * step
    body = pl.ds(COLS, width)

    loads = [
        pltpu.make_async_copy(
            ensemble, extended.at[pl.ds(0, local), pl.ds(EDGE, rows), body], load_sem.at[0]
        ),
        pltpu.make_async_copy(
            velocity, extended.at[pl.ds(local, 2), pl.ds(EDGE, rows), body], load_sem.at[1]
        ),
    ]
    for load in loads:
        load.start()

    barrier = pltpu.get_barrier_semaphore()

    @pl.loop(1, devices)
    def _(k):
        pl.semaphore_signal(barrier, inc=1, device_id={"member": lax.rem(me + k, devices)})

    @pl.when(band > 0)
    def _():
        pl.semaphore_signal(barrier, inc=1, device_id={"tile": band - 1})

    @pl.when(band < bands - 1)
    def _():
        pl.semaphore_signal(barrier, inc=1, device_id={"tile": band + 1})

    extended[:, :, 0:COLS] = jnp.zeros((local + 2, rows + 2 * EDGE, COLS), jnp.float32)
    extended[:, :, COLS + width :] = jnp.zeros((local + 2, rows + 2 * EDGE, COLS), jnp.float32)

    @pl.when(band == 0)
    def _():
        extended[:, 0:EDGE, COLS : COLS + width] = jnp.zeros((local + 2, EDGE, width), jnp.float32)

    @pl.when(band == bands - 1)
    def _():
        extended[:, EDGE + rows :, COLS : COLS + width] = jnp.zeros(
            (local + 2, EDGE, width), jnp.float32
        )

    neighbours = (band > 0).astype(jnp.int32) + (band < bands - 1).astype(jnp.int32)
    pl.semaphore_wait(barrier, devices - 1 + neighbours)

    def halo(side):
        source, target, other = (
            (pl.ds(rows - EDGE, EDGE), pl.ds(0, EDGE), band + 1)
            if side == 0
            else (pl.ds(0, EDGE), pl.ds(EDGE + rows, EDGE), band - 1)
        )
        return [
            pltpu.make_async_remote_copy(
                src_ref=ref.at[:, source, :],
                dst_ref=extended.at[place, target, body],
                send_sem=halo_send.at[side, n],
                recv_sem=halo_recv.at[side, n],
                device_id={"tile": other},
            )
            for n, (ref, place) in enumerate(
                ((ensemble, pl.ds(0, local)), (velocity, pl.ds(local, 2)))
            )
        ]

    has = (band < bands - 1, band > 0)
    for side in range(2):

        @pl.when(has[side])
        def _():
            for copy in halo(side):
                copy.start()

    for load in loads:
        load.wait()

    def far_first(n, place, count):
        half = count // 2
        near_base = (place // half) * half
        base = jnp.where(n < half, half - near_base, near_base)
        return base + lax.rem(place + n, half)

    per_strip = STRIP // COLS
    strips = width // STRIP
    window = step + 2 * EDGE
    reach = STRIP + 2 * COLS

    def forecast(c):
        first = pl.multiple_of(c * step, 8)

        @pl.loop(0, strips)
        def _(turn):
            strip = far_first(turn, me // per_strip, strips)
            lanes = pl.ds(pl.multiple_of(strip * STRIP, COLS), reach)
            span = pl.ds(first, window)
            u = extended[local, span, lanes]
            v = extended[local + 1, span, lanes]

            def nxt(x, axis):
                return pltpu.roll(x, x.shape[axis] - 1, axis)

            def prv(x, axis):
                return pltpu.roll(x, 1, axis)

            a = 0.5 * (u + nxt(u, 0))
            b = 0.5 * (v + nxt(v, 1))
            before_a, before_b = prv(a, 0), prv(b, 1)
            low_a, high_a = jnp.minimum(a, 0.0), jnp.maximum(before_a, 0.0)
            low_b, high_b = jnp.minimum(b, 0.0), jnp.maximum(before_b, 0.0)
            centre = (
                1.0
                - (jnp.maximum(a, 0.0) - jnp.minimum(before_a, 0.0))
                - (jnp.maximum(b, 0.0) - jnp.minimum(before_b, 0.0))
            )
            row = band * rows + c * step - EDGE + lax.broadcasted_iota(jnp.int32, u.shape, 0)
            col = strip * STRIP - COLS + lax.broadcasted_iota(jnp.int32, u.shape, 1)
            inside = (row >= 0) & (row < rows * bands) & (col >= 0) & (col < width)

            def substep(f):
                return (
                    centre * f
                    + (high_a * prv(f, 0) - low_a * nxt(f, 0))
                    + (high_b * prv(f, 1) - low_b * nxt(f, 1))
                )

            for m in range(local):
                f = extended[m, span, lanes]
                f = substep(jnp.where(inside, substep(f), 0.0))
                for h in range(per_strip):
                    outgoing[c, strip * per_strip + h, pl.ds(m * step, step), :] = f[
                        EDGE : EDGE + step, COLS * (1 + h) : COLS * (2 + h)
                    ]

            for h in range(per_strip):
                peer = strip * per_strip + h

                @pl.when(peer == me)
                def _():
                    pltpu.make_async_copy(
                        outgoing.at[c, me], gathered.at[c, pl.ds(me * part, part)], there_own.at[c]
                    ).start()

                @pl.when(peer != me)
                def _():
                    pltpu.make_async_remote_copy(
                        src_ref=outgoing.at[c, peer],
                        dst_ref=gathered.at[c, pl.ds(me * part, part)],
                        send_sem=there_send.at[c],
                        recv_sem=there_recv.at[c],
                        device_id={"member": peer},
                    ).start()

    @pl.loop(1, chunks - 1)
    def _(c):
        forecast(c)

    for side in range(2):

        @pl.when(has[1 - side])
        def _():
            for copy in halo(side):
                copy.wait_recv()

    @pl.loop(0, 2)
    def _(k):
        forecast(k * (chunks - 1))

    def spread_lanes(x):
        return jnp.concatenate([x] * (COLS // slots), axis=1)

    lane = lax.broadcasted_iota(jnp.int32, (rows, COLS), 1)
    parity = lax.broadcasted_iota(jnp.int32, (rows, COLS), 0) % 2
    slot = lane % slots
    mine = (lane // slots) == parity
    columns = spread_lanes(columns_ref[...].T)
    square = (rows, rows)
    diagonal = lax.broadcasted_iota(jnp.int32, square, 0) == lax.broadcasted_iota(
        jnp.int32, square, 1
    )

    def upright(ref):
        line = jnp.broadcast_to(ref[...].astype(jnp.float32), square)
        return jnp.sum(jnp.where(diagonal, line, 0.0), axis=1, keepdims=True)

    live = mine & (slot.astype(jnp.float32) < upright(count_ref))
    offset = (columns.astype(jnp.float32) - 0.5 * (COLS - 1)) / upright(radius_ref)
    weight = 1.0 / (1.0 + offset * offset) / spread_lanes(variance_ref[...].T)
    column_lanes[...] = jnp.where(mine, columns, -1)
    weight_lanes[...] = jnp.where(live, weight, 0.0)
    value_lanes[...] = jnp.where(mine, spread_lanes(value_ref[...].T), 0.0)

    two = 2 * members
    row_index = lax.broadcasted_iota(jnp.int32, (two, two), 0)
    col_index = lax.broadcasted_iota(jnp.int32, (two, two), 1)
    identity = (row_index == col_index).astype(jnp.float32)
    upper = lax.broadcasted_iota(jnp.int32, (two, 1), 0) < members
    sublane = lax.broadcasted_iota(jnp.int32, (COLS, COLS), 0)
    across = (((1,), (1,)), ((), ()))

    def analyse(c, base):
        pairs = []
        for n in range(PAIRS):
            halves, seen, means, weight, value, averages = [], [], [], 0.0, 0.0, []
            for h in range(2):
                r = base + 2 * n + h
                tile_row = c * step + r
                x = gathered[c, pl.ds(r, members, stride=step), :]
                average = jnp.sum(x, axis=0, keepdims=True) * (1.0 / members)
                anomaly = x - average
                hit = (column_lanes[pl.ds(tile_row, 1), :] == sublane).astype(jnp.float32)
                hit = hit.astype(jnp.bfloat16)
                both = jnp.concatenate(
                    [anomaly, jnp.broadcast_to(average, (8, COLS))], axis=0
                )
                high, low = split(both)
                picked = jnp.dot(high, hit, preferred_element_type=jnp.float32) + jnp.dot(
                    low, hit, preferred_element_type=jnp.float32
                )
                halves.append(anomaly)
                averages.append(average)
                seen.append(picked[0:members])
                means.append(picked[members : members + 1])
                weight = weight + weight_lanes[pl.ds(tile_row, 1), :]
                value = value + value_lanes[pl.ds(tile_row, 1), :]
            spread = jnp.concatenate(seen, axis=0)
            scaled = spread * weight
            projected = jnp.sum(
                scaled * (value - (means[0] + means[1])), axis=1, keepdims=True
            )
            pairs.append((halves, averages, spread, scaled, projected))

        systems = [
            product(split(scaled), split(spread), across) + (members - 1.0) * identity
            for _, _, spread, scaled, _ in pairs
        ]
        norms = []
        for system in systems:
            squares = jnp.sum(system * system, axis=1, keepdims=True)
            norms.append(
                jnp.sqrt(
                    jnp.where(
                        upper,
                        jnp.sum(squares[0:members], axis=0, keepdims=True),
                        jnp.sum(squares[members:], axis=0, keepdims=True),
                    )
                )
            )
        roots = [system / norm for system, norm in zip(systems, norms)]
        inverses = [None] * PAIRS
        for sweep in range(SWEEPS):
            if sweep == 0:
                factors = [1.5 * identity - 0.5 * root for root in roots]
                inverses = factors
                parts = [split(factor) for factor in factors]
                inverse_parts = parts
                root_parts = [split(root) for root in roots]
            else:
                factors = [
                    1.5 * identity - 0.5 * product(z, y)
                    for z, y in zip(inverse_parts, root_parts)
                ]
                parts = [split(factor) for factor in factors]
                inverses = [product(p, z) for p, z in zip(parts, inverse_parts)]
                inverse_parts = [split(z) for z in inverses]
            if sweep < SWEEPS - 1:
                roots = [product(y, p) for y, p in zip(root_parts, parts)]
                root_parts = [split(y) for y in roots]
        for n in range(PAIRS):
            halves, averages, _, _, projected = pairs[n]
            inverse = inverses[n] * lax.rsqrt(norms[n])
            halfway = jnp.sum(inverse * projected, axis=0, keepdims=True)
            mean_weight = jnp.sum(inverse * halfway, axis=1, keepdims=True)
            anomaly = jnp.concatenate(halves, axis=0)
            moved = product(split(math.sqrt(members - 1.0) * inverse), split(anomaly))
            shift = mean_weight * anomaly
            for h in range(2):
                inner = slice(h * members, (h + 1) * members)
                centre = averages[h] + jnp.sum(shift[inner], axis=0, keepdims=True)
                analysed[c, pl.ds(base + 2 * n + h, members, stride=step), :] = (
                    moved[inner] + centre
                )

    group_rows = 2 * PAIRS

    def back(c, group, peer):
        return [
            pltpu.make_async_remote_copy(
                src_ref=analysed.at[
                    c,
                    pl.ds(
                        pl.multiple_of(peer * part + m * step + group * group_rows, 8),
                        group_rows,
                    ),
                ],
                dst_ref=out.at[
                    m,
                    pl.ds(pl.multiple_of(c * step + group * group_rows, 8), group_rows),
                    pl.ds(pl.multiple_of(me * COLS, COLS), COLS),
                ],
                send_sem=back_send.at[c],
                recv_sem=back_recv.at[c],
                device_id={"member": peer},
            )
            for m in range(local)
        ]

    def keep(c):
        return [
            pltpu.make_async_copy(
                analysed.at[c, pl.ds(me * part + m * step, step)],
                out.at[
                    m,
                    pl.ds(pl.multiple_of(c * step, 8), step),
                    pl.ds(pl.multiple_of(me * COLS, COLS), COLS),
                ],
                back_own.at[c, m],
            )
            for m in range(local)
        ]

    others = (devices - 1) * part

    def whole(ref, c, sem):
        piece = ref.at[c, pl.ds(0, others)]
        return pltpu.make_async_copy(piece, piece, sem.at[c])

    @pl.loop(0, chunks)
    def _(k):
        c = jnp.where(
            k < chunks - 2, k + 1, (k - (chunks - 2)) * (chunks - 1)
        )
        pltpu.make_async_copy(
            outgoing.at[c, me], gathered.at[c, pl.ds(me * part, part)], there_own.at[c]
        ).wait()
        whole(gathered, c, there_recv).wait()

        @pl.loop(0, step // group_rows)
        def _(group):
            analyse(c, group * group_rows)

            @pl.loop(0, devices)
            def _(turn):
                peer = far_first(turn, me, devices)

                @pl.when(peer != me)
                def _():
                    for copy in back(c, group, peer):
                        copy.start()

        for copy in keep(c):
            copy.start()

    for side in range(2):

        @pl.when(has[side])
        def _():
            for copy in halo(side):
                copy.wait_send()

    @pl.loop(0, chunks)
    def _(c):
        whole(gathered, c, there_send).wait()
        whole(analysed, c, back_send).wait()
        for copy in keep(c):
            copy.wait()
        landed = out.at[
            :, pl.ds(pl.multiple_of(c * step, 8), step), pl.ds(0, (devices - 1) * COLS)
        ]
        pltpu.make_async_copy(landed, landed, back_recv.at[c]).wait()


def place(source, out, staged, in_sem, out_sem):
    local, rows, _ = source.shape
    piece = rows // 2
    spots = [(m, pl.ds(h * piece, piece)) for m in range(local) for h in range(2)]
    reads = [
        pltpu.make_async_copy(source.at[spot], staged.at[spot], in_sem.at[n])
        for n, spot in enumerate(spots)
    ]
    writes = [
        pltpu.make_async_copy(staged.at[spot], out.at[spot], out_sem.at[n])
        for n, spot in enumerate(spots)
    ]
    for read in reads:
        read.start()
    for read, write in zip(reads, writes):
        read.wait()
        write.start()
    for write in writes:
        write.wait()


def per_device(
    ensemble,
    velocity,
    observed_column,
    observation_slot_count,
    local_radius,
    observed_value,
    error_variance,
):
    devices, bands = lax.axis_size("member"), lax.axis_size("tile")
    local, rows, width = ensemble.shape
    slots = observed_column.shape[2]
    step = ROWS_PER_CHUNK
    chunks = rows // step
    part = local * step
    members = devices * local
    sizes = (devices, bands, local, rows, width, step, slots)
    vmem = pl.BlockSpec(memory_space=pltpu.VMEM)
    anywhere = pl.BlockSpec(memory_space=pl.ANY)
    dma = pltpu.SemaphoreType.DMA
    analysis = pl.pallas_call(
        functools.partial(kernel, sizes),
        out_shape=jax.ShapeDtypeStruct(ensemble.shape, jnp.float32),
        in_specs=[anywhere] * 2 + [vmem] * 5,
        out_specs=anywhere,
        scratch_shapes=[
            pltpu.VMEM((local + 2, rows + 2 * EDGE, width + 2 * COLS), jnp.float32),
            pltpu.VMEM((chunks, devices, part, COLS), jnp.float32),
            pltpu.VMEM((chunks, members * step, COLS), jnp.float32),
            pltpu.VMEM((chunks, members * step, COLS), jnp.float32),
            pltpu.VMEM((rows, COLS), jnp.int32),
            pltpu.VMEM((rows, COLS), jnp.float32),
            pltpu.VMEM((rows, COLS), jnp.float32),
            dma((2,)),
            dma((2, 2)),
            dma((2, 2)),
            dma((chunks,)),
            dma((chunks,)),
            dma((chunks,)),
            dma((chunks,)),
            dma((chunks,)),
            dma((chunks, local)),
        ],
        compiler_params=pltpu.CompilerParams(
            collective_id=0, has_side_effects=True, vmem_limit_bytes=62 * 1024 * 1024
        ),
    )(
        ensemble,
        velocity,
        observed_column.reshape(rows, slots).T,
        observation_slot_count.reshape(1, rows),
        local_radius.reshape(1, rows),
        observed_value.reshape(rows, slots).T,
        error_variance.reshape(rows, slots).T,
    )
    return pl.pallas_call(
        place,
        out_shape=jax.ShapeDtypeStruct(ensemble.shape, jnp.float32),
        in_specs=[anywhere],
        out_specs=anywhere,
        scratch_shapes=[
            pltpu.VMEM(ensemble.shape, jnp.float32),
            dma((2 * local,)),
            dma((2 * local,)),
        ],
        compiler_params=pltpu.CompilerParams(vmem_limit_bytes=62 * 1024 * 1024),
    )(analysis)


def solution(mesh):
    placed = (
        P("member", "tile", None),
        P(None, "tile", None),
        P("tile", "member", None),
        P("tile", "member"),
        P("tile", "member"),
        P("tile", "member", None),
        P("tile", "member", None),
    )
    return jax.shard_map(
        per_device, mesh=mesh, in_specs=placed, out_specs=P("member", "tile", None), check_vma=False
    )
```

```python
import functools
import math

import jax
import jax.numpy as jnp
from jax import lax
from jax.experimental import pallas as pl
from jax.experimental.pallas import tpu as pltpu
from jax.sharding import PartitionSpec as P

COLS = 128
SWEEPS = 6
EDGE = 8
STRIP = 256
ROWS_PER_CHUNK = 8
PAIRS = 4


def split(x):
    high = x.astype(jnp.bfloat16)
    low = (x - high.astype(jnp.float32)).astype(jnp.bfloat16)
    return high, low


def product(a, b, dims=(((1,), (0,)), ((), ()))):
    dot = functools.partial(
        lax.dot_general, dimension_numbers=dims, preferred_element_type=jnp.float32
    )
    return dot(a[0], b[0]) + (dot(a[0], b[1]) + dot(a[1], b[0]))


def kernel(
    sizes,
    ensemble,
    velocity,
    columns_ref,
    count_ref,
    radius_ref,
    value_ref,
    variance_ref,
    out,
    extended,
    outgoing,
    gathered,
    analysed,
    column_lanes,
    weight_lanes,
    value_lanes,
    load_sem,
    halo_send,
    halo_recv,
    there_send,
    there_recv,
    there_own,
    back_send,
    back_recv,
    back_own,
):
    devices, bands, local, rows, width, step, slots = sizes
    members = devices * local
    chunks = rows // step
    me = lax.axis_index("member")
    band = lax.axis_index("tile")
    part = local * step
    body = pl.ds(COLS, width)

    loads = [
        pltpu.make_async_copy(
            ensemble, extended.at[pl.ds(0, local), pl.ds(EDGE, rows), body], load_sem.at[0]
        ),
        pltpu.make_async_copy(
            velocity, extended.at[pl.ds(local, 2), pl.ds(EDGE, rows), body], load_sem.at[1]
        ),
    ]
    for load in loads:
        load.start()

    barrier = pltpu.get_barrier_semaphore()

    @pl.loop(1, devices)
    def _(k):
        pl.semaphore_signal(barrier, inc=1, device_id={"member": lax.rem(me + k, devices)})

    @pl.when(band > 0)
    def _():
        pl.semaphore_signal(barrier, inc=1, device_id={"tile": band - 1})

    @pl.when(band < bands - 1)
    def _():
        pl.semaphore_signal(barrier, inc=1, device_id={"tile": band + 1})

    extended[:, :, 0:COLS] = jnp.zeros((local + 2, rows + 2 * EDGE, COLS), jnp.float32)
    extended[:, :, COLS + width :] = jnp.zeros((local + 2, rows + 2 * EDGE, COLS), jnp.float32)

    @pl.when(band == 0)
    def _():
        extended[:, 0:EDGE, COLS : COLS + width] = jnp.zeros((local + 2, EDGE, width), jnp.float32)

    @pl.when(band == bands - 1)
    def _():
        extended[:, EDGE + rows :, COLS : COLS + width] = jnp.zeros(
            (local + 2, EDGE, width), jnp.float32
        )

    neighbours = (band > 0).astype(jnp.int32) + (band < bands - 1).astype(jnp.int32)
    pl.semaphore_wait(barrier, devices - 1 + neighbours)

    def halo(side):
        source, target, other = (
            (pl.ds(rows - EDGE, EDGE), pl.ds(0, EDGE), band + 1)
            if side == 0
            else (pl.ds(0, EDGE), pl.ds(EDGE + rows, EDGE), band - 1)
        )
        return [
            pltpu.make_async_remote_copy(
                src_ref=ref.at[:, source, :],
                dst_ref=extended.at[place, target, body],
                send_sem=halo_send.at[side, n],
                recv_sem=halo_recv.at[side, n],
                device_id={"tile": other},
            )
            for n, (ref, place) in enumerate(
                ((ensemble, pl.ds(0, local)), (velocity, pl.ds(local, 2)))
            )
        ]

    has = (band < bands - 1, band > 0)
    for side in range(2):

        @pl.when(has[side])
        def _():
            for copy in halo(side):
                copy.start()

    for load in loads:
        load.wait()

    def far_first(n, place, count):
        half = count // 2
        near_base = (place // half) * half
        base = jnp.where(n < half, half - near_base, near_base)
        return base + lax.rem(place + n, half)

    per_strip = STRIP // COLS
    strips = width // STRIP
    window = step + 2 * EDGE
    reach = STRIP + 2 * COLS

    def forecast(c):
        first = pl.multiple_of(c * step, 8)

        @pl.loop(0, strips)
        def _(turn):
            strip = far_first(turn, me // per_strip, strips)
            lanes = pl.ds(pl.multiple_of(strip * STRIP, COLS), reach)
            span = pl.ds(first, window)
            u = extended[local, span, lanes]
            v = extended[local + 1, span, lanes]

            def nxt(x, axis):
                return pltpu.roll(x, x.shape[axis] - 1, axis)

            def prv(x, axis):
                return pltpu.roll(x, 1, axis)

            a = 0.5 * (u + nxt(u, 0))
            b = 0.5 * (v + nxt(v, 1))
            before_a, before_b = prv(a, 0), prv(b, 1)
            low_a, high_a = jnp.minimum(a, 0.0), jnp.maximum(before_a, 0.0)
            low_b, high_b = jnp.minimum(b, 0.0), jnp.maximum(before_b, 0.0)
            centre = (
                1.0
                - (jnp.maximum(a, 0.0) - jnp.minimum(before_a, 0.0))
                - (jnp.maximum(b, 0.0) - jnp.minimum(before_b, 0.0))
            )
            row = band * rows + c * step - EDGE + lax.broadcasted_iota(jnp.int32, u.shape, 0)
            col = strip * STRIP - COLS + lax.broadcasted_iota(jnp.int32, u.shape, 1)
            inside = (row >= 0) & (row < rows * bands) & (col >= 0) & (col < width)

            def substep(f):
                return (
                    centre * f
                    + (high_a * prv(f, 0) - low_a * nxt(f, 0))
                    + (high_b * prv(f, 1) - low_b * nxt(f, 1))
                )

            for m in range(local):
                f = extended[m, span, lanes]
                f = substep(jnp.where(inside, substep(f), 0.0))
                for h in range(per_strip):
                    outgoing[c, strip * per_strip + h, pl.ds(m * step, step), :] = f[
                        EDGE : EDGE + step, COLS * (1 + h) : COLS * (2 + h)
                    ]

            for h in range(per_strip):
                peer = strip * per_strip + h

                @pl.when(peer == me)
                def _():
                    pltpu.make_async_copy(
                        outgoing.at[c, me], gathered.at[c, pl.ds(me * part, part)], there_own.at[c]
                    ).start()

                @pl.when(peer != me)
                def _():
                    pltpu.make_async_remote_copy(
                        src_ref=outgoing.at[c, peer],
                        dst_ref=gathered.at[c, pl.ds(me * part, part)],
                        send_sem=there_send.at[c],
                        recv_sem=there_recv.at[c],
                        device_id={"member": peer},
                    ).start()

    @pl.loop(1, chunks - 1)
    def _(c):
        forecast(c)

    for side in range(2):

        @pl.when(has[1 - side])
        def _():
            for copy in halo(side):
                copy.wait_recv()

    @pl.loop(0, 2)
    def _(k):
        forecast(k * (chunks - 1))

    def spread_lanes(x):
        return jnp.concatenate([x] * (COLS // slots), axis=1)

    lane = lax.broadcasted_iota(jnp.int32, (rows, COLS), 1)
    parity = lax.broadcasted_iota(jnp.int32, (rows, COLS), 0) % 2
    slot = lane % slots
    mine = (lane // slots) == parity
    columns = spread_lanes(columns_ref[...].T)
    square = (rows, rows)
    diagonal = lax.broadcasted_iota(jnp.int32, square, 0) == lax.broadcasted_iota(
        jnp.int32, square, 1
    )

    def upright(ref):
        line = jnp.broadcast_to(ref[...].astype(jnp.float32), square)
        return jnp.sum(jnp.where(diagonal, line, 0.0), axis=1, keepdims=True)

    live = mine & (slot.astype(jnp.float32) < upright(count_ref))
    offset = (columns.astype(jnp.float32) - 0.5 * (COLS - 1)) / upright(radius_ref)
    weight = 1.0 / (1.0 + offset * offset) / spread_lanes(variance_ref[...].T)
    column_lanes[...] = jnp.where(mine, columns, -1)
    weight_lanes[...] = jnp.where(live, weight, 0.0)
    value_lanes[...] = jnp.where(mine, spread_lanes(value_ref[...].T), 0.0)

    two = 2 * members
    row_index = lax.broadcasted_iota(jnp.int32, (two, two), 0)
    col_index = lax.broadcasted_iota(jnp.int32, (two, two), 1)
    identity = (row_index == col_index).astype(jnp.float32)
    upper = lax.broadcasted_iota(jnp.int32, (two, 1), 0) < members
    sublane = lax.broadcasted_iota(jnp.int32, (COLS, COLS), 0)
    across = (((1,), (1,)), ((), ()))

    def analyse(c, base):
        pairs = []
        for n in range(PAIRS):
            halves, seen, means, weight, value, averages = [], [], [], 0.0, 0.0, []
            for h in range(2):
                r = base + 2 * n + h
                tile_row = c * step + r
                x = gathered[c, pl.ds(r, members, stride=step), :]
                average = jnp.sum(x, axis=0, keepdims=True) * (1.0 / members)
                anomaly = x - average
                hit = (column_lanes[pl.ds(tile_row, 1), :] == sublane).astype(jnp.float32)
                hit = hit.astype(jnp.bfloat16)
                both = jnp.concatenate(
                    [anomaly, jnp.broadcast_to(average, (8, COLS))], axis=0
                )
                high, low = split(both)
                picked = jnp.dot(high, hit, preferred_element_type=jnp.float32) + jnp.dot(
                    low, hit, preferred_element_type=jnp.float32
                )
                halves.append(anomaly)
                averages.append(average)
                seen.append(picked[0:members])
                means.append(picked[members : members + 1])
                weight = weight + weight_lanes[pl.ds(tile_row, 1), :]
                value = value + value_lanes[pl.ds(tile_row, 1), :]
            spread = jnp.concatenate(seen, axis=0)
            scaled = spread * weight
            projected = jnp.sum(
                scaled * (value - (means[0] + means[1])), axis=1, keepdims=True
            )
            pairs.append((halves, averages, spread, scaled, projected))

        systems = [
            product(split(scaled), split(spread), across) + (members - 1.0) * identity
            for _, _, spread, scaled, _ in pairs
        ]
        norms = []
        for system in systems:
            squares = jnp.sum(system * system, axis=1, keepdims=True)
            norms.append(
                jnp.sqrt(
                    jnp.where(
                        upper,
                        jnp.sum(squares[0:members], axis=0, keepdims=True),
                        jnp.sum(squares[members:], axis=0, keepdims=True),
                    )
                )
            )
        roots = [system / norm for system, norm in zip(systems, norms)]
        inverses = [None] * PAIRS
        for sweep in range(SWEEPS):
            if sweep == 0:
                factors = [1.5 * identity - 0.5 * root for root in roots]
                inverses = factors
                parts = [split(factor) for factor in factors]
                inverse_parts = parts
                root_parts = [split(root) for root in roots]
            else:
                factors = [
                    1.5 * identity - 0.5 * product(z, y)
                    for z, y in zip(inverse_parts, root_parts)
                ]
                parts = [split(factor) for factor in factors]
                inverses = [product(p, z) for p, z in zip(parts, inverse_parts)]
                inverse_parts = [split(z) for z in inverses]
            if sweep < SWEEPS - 1:
                roots = [product(y, p) for y, p in zip(root_parts, parts)]
                root_parts = [split(y) for y in roots]
        for n in range(PAIRS):
            halves, averages, _, _, projected = pairs[n]
            inverse = inverses[n] * lax.rsqrt(norms[n])
            halfway = jnp.sum(inverse * projected, axis=0, keepdims=True)
            mean_weight = jnp.sum(inverse * halfway, axis=1, keepdims=True)
            anomaly = jnp.concatenate(halves, axis=0)
            moved = product(split(math.sqrt(members - 1.0) * inverse), split(anomaly))
            shift = mean_weight * anomaly
            for h in range(2):
                inner = slice(h * members, (h + 1) * members)
                centre = averages[h] + jnp.sum(shift[inner], axis=0, keepdims=True)
                analysed[c, pl.ds(base + 2 * n + h, members, stride=step), :] = (
                    moved[inner] + centre
                )

    group_rows = 2 * PAIRS

    def back(c, group, peer):
        return [
            pltpu.make_async_remote_copy(
                src_ref=analysed.at[
                    c,
                    pl.ds(
                        pl.multiple_of(peer * part + m * step + group * group_rows, 8),
                        group_rows,
                    ),
                ],
                dst_ref=out.at[
                    m,
                    pl.ds(pl.multiple_of(c * step + group * group_rows, 8), group_rows),
                    pl.ds(pl.multiple_of(me * COLS, COLS), COLS),
                ],
                send_sem=back_send.at[c],
                recv_sem=back_recv.at[c],
                device_id={"member": peer},
            )
            for m in range(local)
        ]

    def keep(c):
        return [
            pltpu.make_async_copy(
                analysed.at[c, pl.ds(me * part + m * step, step)],
                out.at[
                    m,
                    pl.ds(pl.multiple_of(c * step, 8), step),
                    pl.ds(pl.multiple_of(me * COLS, COLS), COLS),
                ],
                back_own.at[c, m],
            )
            for m in range(local)
        ]

    others = (devices - 1) * part

    def whole(ref, c, sem):
        piece = ref.at[c, pl.ds(0, others)]
        return pltpu.make_async_copy(piece, piece, sem.at[c])

    @pl.loop(0, chunks)
    def _(k):
        c = jnp.where(
            k < chunks - 2, k + 1, (k - (chunks - 2)) * (chunks - 1)
        )
        pltpu.make_async_copy(
            outgoing.at[c, me], gathered.at[c, pl.ds(me * part, part)], there_own.at[c]
        ).wait()
        whole(gathered, c, there_recv).wait()

        @pl.loop(0, step // group_rows)
        def _(group):
            analyse(c, group * group_rows)

            @pl.loop(0, devices)
            def _(turn):
                peer = far_first(turn, me, devices)

                @pl.when(peer != me)
                def _():
                    for copy in back(c, group, peer):
                        copy.start()

        for copy in keep(c):
            copy.start()

    for side in range(2):

        @pl.when(has[side])
        def _():
            for copy in halo(side):
                copy.wait_send()

    @pl.loop(0, chunks)
    def _(c):
        whole(gathered, c, there_send).wait()
        whole(analysed, c, back_send).wait()
        for copy in keep(c):
            copy.wait()
        landed = out.at[
            :, pl.ds(pl.multiple_of(c * step, 8), step), pl.ds(0, (devices - 1) * COLS)
        ]
        pltpu.make_async_copy(landed, landed, back_recv.at[c]).wait()


def place(source, out, staged, in_sem, out_sem):
    local, rows, _ = source.shape
    piece = rows // 2
    spots = [(m, pl.ds(h * piece, piece)) for m in range(local) for h in range(2)]
    reads = [
        pltpu.make_async_copy(source.at[spot], staged.at[spot], in_sem.at[n])
        for n, spot in enumerate(spots)
    ]
    writes = [
        pltpu.make_async_copy(staged.at[spot], out.at[spot], out_sem.at[n])
        for n, spot in enumerate(spots)
    ]
    for read in reads:
        read.start()
    for read, write in zip(reads, writes):
        read.wait()
        write.start()
    for write in writes:
        write.wait()


def per_device(
    ensemble,
    velocity,
    observed_column,
    observation_slot_count,
    local_radius,
    observed_value,
    error_variance,
):
    devices, bands = lax.axis_size("member"), lax.axis_size("tile")
    local, rows, width = ensemble.shape
    slots = observed_column.shape[2]
    step = ROWS_PER_CHUNK
    chunks = rows // step
    part = local * step
    members = devices * local
    sizes = (devices, bands, local, rows, width, step, slots)
    vmem = pl.BlockSpec(memory_space=pltpu.VMEM)
    anywhere = pl.BlockSpec(memory_space=pl.ANY)
    dma = pltpu.SemaphoreType.DMA
    analysis = pl.pallas_call(
        functools.partial(kernel, sizes),
        out_shape=jax.ShapeDtypeStruct(ensemble.shape, jnp.float32),
        in_specs=[anywhere] * 2 + [vmem] * 5,
        out_specs=anywhere,
        scratch_shapes=[
            pltpu.VMEM((local + 2, rows + 2 * EDGE, width + 2 * COLS), jnp.float32),
            pltpu.VMEM((chunks, devices, part, COLS), jnp.float32),
            pltpu.VMEM((chunks, members * step, COLS), jnp.float32),
            pltpu.VMEM((chunks, members * step, COLS), jnp.float32),
            pltpu.VMEM((rows, COLS), jnp.int32),
            pltpu.VMEM((rows, COLS), jnp.float32),
            pltpu.VMEM((rows, COLS), jnp.float32),
            dma((2,)),
            dma((2, 2)),
            dma((2, 2)),
            dma((chunks,)),
            dma((chunks,)),
            dma((chunks,)),
            dma((chunks,)),
            dma((chunks,)),
            dma((chunks, local)),
        ],
        compiler_params=pltpu.CompilerParams(
            collective_id=0, has_side_effects=True, vmem_limit_bytes=62 * 1024 * 1024
        ),
    )(
        ensemble,
        velocity,
        observed_column.reshape(rows, slots).T,
        observation_slot_count.reshape(1, rows),
        local_radius.reshape(1, rows),
        observed_value.reshape(rows, slots).T,
        error_variance.reshape(rows, slots).T,
    )
    return pl.pallas_call(
        place,
        out_shape=jax.ShapeDtypeStruct(ensemble.shape, jnp.float32),
        in_specs=[anywhere],
        out_specs=anywhere,
        scratch_shapes=[
            pltpu.VMEM(ensemble.shape, jnp.float32),
            dma((2 * local,)),
            dma((2 * local,)),
        ],
        compiler_params=pltpu.CompilerParams(vmem_limit_bytes=62 * 1024 * 1024),
    )(analysis)


def solution(mesh):
    placed = (
        P("member", "tile", None),
        P(None, "tile", None),
        P("tile", "member", None),
        P("tile", "member"),
        P("tile", "member"),
        P("tile", "member", None),
        P("tile", "member", None),
    )
    return jax.shard_map(
        per_device, mesh=mesh, in_specs=placed, out_specs=P("member", "tile", None), check_vma=False
    )
```
